32 devices in a mesh: grp: 2 (over y), surf: 4 (over z), ang: 2 (over x), row: 2 (over core).
Axes of the slice: x: 2, y: 2, z: 4, core: 2. Of those that a mesh axis runs over, the one named last changes fastest.
Arguments:
- incident: bfloat16 [256, 32768], P(('grp', 'ang'), 'surf'), parts along dimension 0, may hold values from -6 to 6
- near_blocks: bfloat16 [512, 4, 128, 128], P(('grp', 'surf', 'row')), parts along dimension 0, may hold values from -0.25 to 0.25
- near_cols: int32 [512, 4], P(('grp', 'surf', 'row')), parts along dimension 0, may hold values from 0 to 95
- gram_inv: bfloat16 [512, 128, 128], P(('grp', 'surf', 'row')), parts along dimension 0, may hold values from -0.5 to 0.5
- prolong: bfloat16 [512, 128, 768], P(('grp', 'surf')), parts along dimension 0, may hold values from -0.5 to 0.5
- dual_blocks: bfloat16 [3072, 3, 128, 128], P(('grp', 'surf', 'row')), parts along dimension 0, may hold values from -0.3125 to 0.3125
- dual_cols: int32 [3072, 3], P(('grp', 'surf', 'row')), parts along dimension 0, may hold values from 0 to 575
- dual_count: int32 [3072], P(('grp', 'surf', 'row')), parts along dimension 0, may hold values from 1 to 3, as said below
- primal_border: int32 [8, 2, 16], P(('grp', 'surf')), parts along dimension 0, may hold values from 0 to 63, as said below
- fine_border: int32 [8, 2, 96], P(('grp', 'surf')), parts along dimension 0, may hold values from 0 to 383, as said below
Outputs:
- preconditioned: float32 [256, 32768], P(('grp', 'ang'), ('surf', 'row')), parts along dimension 0
The draws below stay inside these ranges and needn't reach their ends.
There are 2 independent parts, one for each index of `grp`. The reference program is written for one: setup_inputs(seed, part) draws one part's arguments, and reference() takes and returns one part's arrays. A program takes and returns all parts, laid end to end along the dimension named above; each array names one. Nothing has to cross between parts.
Inputs may be any that keep to these rules, and one draw needn't show every extreme that they name: near_cols indexes the 64 own blocks, then the 16 received from the partition before, then the 16 from the one after. dual_cols indexes the 384 own fine blocks, then the 96 received from the partition before, then the 96 from the one after. Only the first dual_count[f] blocks and column indices of row f count; every half of a partition's fine rows has a row with 3. `primal_border`: the 32 blocks listed for one partition are distinct. `fine_border`: the 192 fine blocks listed for one partition are distinct.
All inputs are finite; a program needn't handle non-finite values.
Results may differ from the reference program's by a relative error of at most 0.0064.
Values may be sent and summed in bfloat16 or wider, within the bound.
A program may use at most 192 MiB of HBM per device.

```python
import jax
import jax.numpy as jnp
from jax import lax

B = 128
FINE = 6
KN = 4
KD = 3
PB = 64
HB = 16
HF = 96
COLS = 128
NB = 256
NF = 32768
NFB = 1536
N_SURF = 4
N_ROW = 2


def border_lists(key, total, list_width):
    part_keys = jax.random.split(key, N_SURF)
    shuffled = jax.vmap(lambda single_key: jax.random.permutation(single_key, total))(part_keys)
    return shuffled[:, :2 * list_width].reshape(N_SURF, 2, list_width).astype(jnp.int32)


def draw_primal_border(key, part):
    key = jax.random.fold_in(key, 3)
    return border_lists(key, PB, HB)


def draw_fine_border(key, part):
    key = jax.random.fold_in(key, 5)
    return border_lists(key, FINE * PB, HF)


def draw_dual_count(key, part):
    key = jax.random.fold_in(key, 7)
    heavy_key, light_key = jax.random.split(key)
    halves = N_SURF * N_ROW
    per_half = FINE * PB // N_ROW
    heavy_half = jax.random.randint(heavy_key, (halves, 1), 0, 2)
    light_rows = jax.random.randint(light_key, (halves, per_half), 1, KD)
    counts = jnp.where(heavy_half == 1, KD, light_rows)
    first_col = jnp.arange(per_half)[None, :] == 0
    counts = jnp.where(first_col, KD, counts)
    return counts.reshape(-1).astype(jnp.int32)


def touch_ends(array, stream_key, least, largest):
    longest = array.shape.index(max(array.shape))
    spots = []
    for shift in (0, 1):
        where = [jax.random.randint(jax.random.fold_in(stream_key, axis), (), 0, length) for axis, length in enumerate(array.shape)]
        where[longest] = (where[longest] + shift) % array.shape[longest]
        spots.append(tuple(where))
    return array.at[spots[0]].set(least).at[spots[1]].set(largest)


def levels(rng, dims, pieces, least, high):
    def one(dim, parts):
        steps = jax.random.uniform(jax.random.fold_in(jax.random.fold_in(rng, 6), dim), (parts,), jnp.float32, least / len(pieces), high / len(pieces))
        return jnp.repeat(jnp.exp(steps), dims[dim] // parts).reshape((-1,) + (1,) * (len(dims) - dim - 1))

    level = one(*pieces[0])
    for cut in pieces[1:]:
        level = level * one(*cut)
    return level


def gaussian(key, shape, deviation, reach, cuts=(), dtype=jnp.bfloat16):
    array = deviation * jax.random.normal(key, shape, jnp.float32)
    if cuts:
        array = array * levels(key, shape, cuts, -0.22, 0.18)
    return jnp.clip(array, -reach, reach).astype(dtype)


def setup_inputs(seed: int = 0, part: int = 0) -> dict:
    arg_keys = jax.random.split(jax.random.key(seed), 11)
    part_splits = jax.random.split(jax.random.fold_in(arg_keys[10], part), 11)
    return {
        "incident": gaussian(part_splits[0], (COLS, NF), 1.0, 6.0, ((0, 2), (1, 4))),
        "near_blocks": gaussian(part_splits[1], (NB, KN, B, B), (KN * B) ** -0.5, 0.25, ((0, 8),)),
        "near_cols": touch_ends(jax.random.randint(part_splits[2], (NB, KN), 0, PB + 2 * HB), jax.random.fold_in(part_splits[2], 1), 0, (PB + 2 * HB) - 1).astype(jnp.int32),
        "gram_inv": gaussian(part_splits[3], (NB, B, B), B ** -0.5, 0.5, ((0, 8),)),
        "prolong": gaussian(part_splits[4], (NB, B, FINE * B), B ** -0.5, 0.5, ((0, 4),)),
        "dual_blocks": gaussian(part_splits[5], (NFB, KD, B, B), (KD * B) ** -0.5, 0.3125, ((0, 8),)),
        "dual_cols": touch_ends(jax.random.randint(part_splits[6], (NFB, KD), 0, FINE * PB + 2 * HF), jax.random.fold_in(part_splits[6], 1), 0, (FINE * PB + 2 * HF) - 1).astype(jnp.int32),
        "dual_count": draw_dual_count(jax.random.fold_in(jax.random.fold_in(arg_keys[10], part), 71), part),
        "primal_border": draw_primal_border(jax.random.fold_in(jax.random.fold_in(arg_keys[10], part), 71), part),
        "fine_border": draw_fine_border(jax.random.fold_in(jax.random.fold_in(arg_keys[10], part), 71), part),
    }


def with_rims(fields, borders):
    list_width = borders.shape[2]
    chosen = jax.vmap(lambda single, border_rows: jnp.take(single, border_rows.reshape(-1), axis=1))(fields, borders)
    from_before = jnp.roll(chosen[:, :, list_width:], 1, axis=0)
    from_after = jnp.roll(chosen[:, :, :list_width], -1, axis=0)
    return jnp.concatenate([fields, from_before, from_after], axis=2)


def reference(incident, near_blocks, near_cols, gram_inv, prolong, dual_blocks, dual_cols, dual_count, primal_border, fine_border):
    wide = jnp.float32
    by_part = incident.reshape(COLS, N_SURF, PB, B).transpose(1, 0, 2, 3)
    extended = with_rims(by_part, primal_border)
    near_part = near_blocks.reshape(N_SURF, PB, KN, B, B)
    near_index = near_cols.reshape(N_SURF, PB, KN)
    gram_part = gram_inv.reshape(N_SURF, PB, B, B)
    prol_part = prolong.reshape(N_SURF, PB, B, FINE * B)

    def primal_section(packed):
        ext_field, matrices, indices, gram, prol = packed
        picked = jnp.take(ext_field, indices, axis=1).astype(wide)
        applied = jnp.einsum("cikb,ikbe->cie", picked, matrices.astype(wide)).astype(jnp.bfloat16)
        applied = lax.optimization_barrier(applied)
        mapped = jnp.einsum("cib,ibe->cie", applied.astype(wide), gram.astype(wide)).astype(jnp.bfloat16)
        refined = jnp.einsum("cib,ibe->cie", mapped.astype(wide), prol.astype(wide)).astype(jnp.bfloat16)
        return refined.reshape(COLS, PB * FINE, B)

    fine_field = lax.map(primal_section, (extended, near_part, near_index, gram_part, prol_part))
    fine_extended = with_rims(fine_field, fine_border)
    dual_part = dual_blocks.reshape(N_SURF, FINE * PB, KD, B, B)
    dual_index = dual_cols.reshape(N_SURF, FINE * PB, KD)
    count_part = dual_count.reshape(N_SURF, FINE * PB)

    def dual_section(packed):
        ext_field, matrices, indices, counts, gram, prol = packed
        picked = jnp.take(ext_field, indices, axis=1).astype(wide)
        live_mask = jnp.arange(KD)[None, :] < counts[:, None]
        picked = jnp.where(live_mask[None, :, :, None], picked, jnp.zeros((), wide))
        response = jnp.einsum("cfkb,fkbe->cfe", picked, matrices.astype(wide)).astype(jnp.bfloat16)
        collapsed = jnp.einsum("cie,ibe->cib", response.reshape(COLS, PB, FINE * B).astype(wide), prol.astype(wide)).astype(jnp.bfloat16)
        collapsed = lax.optimization_barrier(collapsed)
        result = jnp.einsum("cib,ieb->cie", collapsed.astype(wide), gram.astype(wide))
        return result.reshape(COLS, PB * B)

    outputs = lax.map(dual_section, (fine_extended, dual_part, dual_index, count_part, gram_part, prol_part))
    return outputs.transpose(1, 0, 2).reshape(COLS, N_SURF * PB * B)
```

```python
import functools

import jax
import jax.numpy as jnp
from jax import lax
from jax.experimental import pallas as pl
from jax.experimental.pallas import tpu as pltpu
from jax.sharding import PartitionSpec as P

MESH = pl.DeviceIdType.MESH
CHUNKS = 4


def dot(a, b):
    return jnp.dot(a, b, preferred_element_type=jnp.float32)


def dot_t(a, b):
    return lax.dot_general(a, b, (((1,), (1,)), ((), ())), preferred_element_type=jnp.float32)


def spread(prolong, q):
    return jnp.concatenate([prolong[q, j] for j in range(prolong.shape[1])], axis=1)


def pick(index, live, k, spare):
    if k == 0:
        return index
    return spare + (index - spare) * lax.min(lax.max(live - k, 0), 1)


def kernel(
    parts,
    near_cols,
    dual_cols,
    dual_count,
    primal_border,
    fine_border,
    incident,
    near_hbm,
    gram_hbm,
    prolong_hbm,
    dual_hbm,
    out,
    near,
    gram,
    prolong,
    dual,
    near_field,
    rim_out,
    rim_in,
    mapped,
    fine_out,
    fine,
    load_sem,
    rim_send,
    rim_recv,
    rim_pass_send,
    rim_pass_recv,
    map_send,
    map_recv,
    fine_send,
    fine_recv,
    fine_pass_send,
    fine_pass_recv,
):
    half_rows, near_terms = near_cols.shape
    coarse, per, block, _ = prolong.shape
    terms = dual_cols.shape[1]
    columns = incident.shape[0]
    rim = primal_border.shape[2]
    rim_half = rim // 2
    fine_rim = fine_border.shape[2]
    fine_half = fine_rim // 2
    step = fine_half // CHUNKS
    own_fine = coarse * per
    row = lax.axis_index("row")
    surf = lax.axis_index("surf")
    sibling = {"row": 1 - row}
    neighbours = (
        {"surf": lax.rem(surf + parts - 1, parts)},
        {"surf": lax.rem(surf + 1, parts)},
    )

    moves = [(near_hbm, near), (gram_hbm, gram), (dual_hbm, dual)] + [
        (prolong_hbm.at[:, :, pl.ds(j * block, block)], prolong.at[:, j]) for j in range(per)
    ]
    loads = [
        pltpu.make_async_copy(src, dst, load_sem.at[i]) for i, (src, dst) in enumerate(moves)
    ]
    for load in loads:
        load.start()

    barrier = pltpu.get_barrier_semaphore()
    for device in neighbours + (sibling,):
        pl.semaphore_signal(barrier, inc=1, device_id=device, device_id_type=MESH)

    def lay(j, carry):
        near_field[j] = incident[:, pl.ds(pl.multiple_of(j * block, block), block)]
        return carry

    lax.fori_loop(0, coarse, lay, 0, unroll=4)
    for way in range(2):

        def pack(j, carry, way=way):
            at = primal_border[0, way, row * rim_half + j]
            rim_out[way, j] = near_field[at]
            return carry

        lax.fori_loop(0, rim_half, pack, 0, unroll=True)

    pl.semaphore_wait(barrier, 3)

    rim_copies = [
        pltpu.make_async_remote_copy(
            src_ref=rim_out.at[way],
            dst_ref=rim_in.at[1 - way, row],
            send_sem=rim_send.at[way],
            recv_sem=rim_recv.at[1 - way],
            device_id=neighbours[way],
            device_id_type=MESH,
        )
        for way in range(2)
    ]
    for copy in rim_copies:
        copy.start()

    fine[own_fine + 2 * fine_rim] = jnp.zeros((columns, block), jnp.bfloat16)

    rim_passes = []
    for way in range(2):
        rim_copies[way].wait_recv()
        copy = pltpu.make_async_remote_copy(
            src_ref=rim_in.at[1 - way, row],
            dst_ref=rim_in.at[1 - way, row],
            send_sem=rim_pass_send.at[way],
            recv_sem=rim_pass_recv.at[way],
            device_id=sibling,
            device_id_type=MESH,
        )
        copy.start()
        rim_passes.append(copy)
    for copy in rim_passes:
        copy.wait_recv()
    for side in range(2):
        for half in range(2):
            for j in range(rim_half):
                near_field[coarse + side * rim + half * rim_half + j] = rim_in[side, half, j]

    loads[0].wait()
    loads[1].wait()
    map_copies = []
    map_step = half_rows // CHUNKS
    for chunk in range(CHUNKS):

        def primal(i, carry):
            picked = jnp.concatenate([near_field[near_cols[i, k]] for k in range(near_terms)], axis=1)
            applied = dot(picked, near[i].reshape(near_terms * block, block)).astype(jnp.bfloat16)
            mapped[row * half_rows + i] = dot(applied, gram[i]).astype(jnp.bfloat16)
            return carry

        lax.fori_loop(chunk * map_step, (chunk + 1) * map_step, primal, 0, unroll=4)
        span = pl.ds(row * half_rows + chunk * map_step, map_step)
        copy = pltpu.make_async_remote_copy(
            src_ref=mapped.at[span],
            dst_ref=mapped.at[span],
            send_sem=map_send.at[chunk],
            recv_sem=map_recv.at[chunk],
            device_id=sibling,
            device_id_type=MESH,
        )
        copy.start()
        map_copies.append(copy)

    for load in loads[3:]:
        load.wait()
    for copy in map_copies:
        copy.wait()

    fine_copies = []
    for chunk in range(CHUNKS):
        for way in range(2):

            def border(j, carry, way=way):
                at = fine_border[0, way, row * fine_half + j]
                source = lax.div(at, per)
                fine_out[way, j] = dot(
                    mapped[source], prolong[source, at - source * per]
                ).astype(jnp.bfloat16)
                return carry

            lax.fori_loop(chunk * step, (chunk + 1) * step, border, 0, unroll=4)
            copy = pltpu.make_async_remote_copy(
                src_ref=fine_out.at[way, pl.ds(chunk * step, step)],
                dst_ref=fine.at[
                    pl.ds(own_fine + (1 - way) * fine_rim + row * fine_half + chunk * step, step)
                ],
                send_sem=fine_send.at[way, chunk],
                recv_sem=fine_recv.at[1 - way, chunk],
                device_id=neighbours[way],
                device_id_type=MESH,
            )
            copy.start()
            fine_copies.append((way, chunk, copy))

    def refine(q, carry):
        result = dot(mapped[q], spread(prolong, q)).astype(jnp.bfloat16)
        for j in range(per):
            fine[q * per + j] = result[:, j * block : (j + 1) * block]
        return carry

    lax.fori_loop(0, coarse, refine, 0, unroll=2)
    loads[2].wait()

    fine_passes = []
    for way, chunk, arrived in fine_copies:
        arrived.wait_recv()
        span = pl.ds(own_fine + (1 - way) * fine_rim + row * fine_half + chunk * step, step)
        copy = pltpu.make_async_remote_copy(
            src_ref=fine.at[span],
            dst_ref=fine.at[span],
            send_sem=fine_pass_send.at[way, chunk],
            recv_sem=fine_pass_recv.at[way, chunk],
            device_id=sibling,
            device_id_type=MESH,
        )
        copy.start()
        fine_passes.append(copy)
    for copy in fine_passes:
        copy.wait()

    def collapse(i, carry):
        pieces = []
        for j in range(per):
            f = i * per + j
            live = dual_count[f]
            picked = jnp.concatenate(
                [
                    fine[pick(dual_cols[f, k], live, k, own_fine + 2 * fine_rim)]
                    for k in range(terms)
                ],
                axis=1,
            )
            pieces.append(dot(picked, dual[f].reshape(terms * block, block)).astype(jnp.bfloat16))
        response = jnp.concatenate(pieces, axis=1)
        collapsed = dot_t(response, spread(prolong, row * half_rows + i)).astype(jnp.bfloat16)
        out[:, pl.ds(pl.multiple_of(i * block, block), block)] = dot_t(collapsed, gram[i])
        return carry

    lax.fori_loop(0, half_rows, collapse, 0, unroll=2)

    for copy in rim_copies + rim_passes:
        copy.wait_send()
    for _, _, copy in fine_copies:
        copy.wait_send()


def body(
    parts,
    incident,
    near_blocks,
    near_cols,
    gram_inv,
    prolong,
    dual_blocks,
    dual_cols,
    dual_count,
    primal_border,
    fine_border,
):
    columns = incident.shape[0]
    coarse, block, wide = prolong.shape
    per = wide // block
    half_rows = near_blocks.shape[0]
    rim = primal_border.shape[2]
    fine_rim = fine_border.shape[2]
    cell = (columns, block)
    low = jnp.bfloat16
    smem = pl.BlockSpec(memory_space=pltpu.SMEM)
    vmem = pl.BlockSpec(memory_space=pltpu.VMEM)
    hbm = pl.BlockSpec(memory_space=pl.ANY)
    sems = pltpu.SemaphoreType.DMA
    return pl.pallas_call(
        functools.partial(kernel, parts),
        out_shape=jax.ShapeDtypeStruct((columns, half_rows * block), jnp.float32),
        in_specs=[smem] * 5 + [vmem] + [hbm] * 4,
        out_specs=vmem,
        scratch_shapes=[
            pltpu.VMEM(near_blocks.shape, low),
            pltpu.VMEM(gram_inv.shape, low),
            pltpu.VMEM((coarse, per, block, block), low),
            pltpu.VMEM(dual_blocks.shape, low),
            pltpu.VMEM((coarse + 2 * rim,) + cell, low),
            pltpu.VMEM((2, rim // 2) + cell, low),
            pltpu.VMEM((2, 2, rim // 2) + cell, low),
            pltpu.VMEM((coarse,) + cell, low),
            pltpu.VMEM((2, fine_rim // 2) + cell, low),
            pltpu.VMEM((coarse * per + 2 * fine_rim + 1,) + cell, low),
            sems((3 + per,)),
            sems((2,)),
            sems((2,)),
            sems((2,)),
            sems((2,)),
            sems((CHUNKS,)),
            sems((CHUNKS,)),
            sems((2, CHUNKS)),
            sems((2, CHUNKS)),
            sems((2, CHUNKS)),
            sems((2, CHUNKS)),
        ],
        compiler_params=pltpu.CompilerParams(
            collective_id=0, has_side_effects=True, vmem_limit_bytes=60 * 2**20
        ),
    )(
        near_cols,
        dual_cols,
        dual_count,
        primal_border,
        fine_border,
        incident,
        near_blocks,
        gram_inv,
        prolong,
        dual_blocks,
    )


def solution(mesh):
    return jax.shard_map(
        functools.partial(body, mesh.shape["surf"]),
        mesh=mesh,
        in_specs=(
            P(("grp", "ang"), "surf"),
            P(("grp", "surf", "row"), None, None, None),
            P(("grp", "surf", "row"), None),
            P(("grp", "surf", "row"), None, None),
            P(("grp", "surf"), None, None),
            P(("grp", "surf", "row"), None, None, None),
            P(("grp", "surf", "row"), None),
            P(("grp", "surf", "row")),
            P(("grp", "surf"), None, None),
            P(("grp", "surf"), None, None),
        ),
        out_specs=P(("grp", "ang"), ("surf", "row")),
        check_vma=False,
    )
```

```python
import functools

import jax
import jax.numpy as jnp
from jax import lax
from jax.experimental import pallas as pl
from jax.experimental.pallas import tpu as pltpu
from jax.sharding import PartitionSpec as P

MESH = pl.DeviceIdType.MESH
CHUNKS = 4


def dot(a, b):
    return jnp.dot(a, b, preferred_element_type=jnp.float32)


def dot_t(a, b):
    return lax.dot_general(a, b, (((1,), (1,)), ((), ())), preferred_element_type=jnp.float32)


def spread(prolong, q):
    return jnp.concatenate([prolong[q, j] for j in range(prolong.shape[1])], axis=1)


def pick(index, live, k, spare):
    if k == 0:
        return index
    return spare + (index - spare) * lax.min(lax.max(live - k, 0), 1)


def kernel(
    parts,
    near_cols,
    dual_cols,
    dual_count,
    primal_border,
    fine_border,
    incident,
    near_hbm,
    gram_hbm,
    prolong_hbm,
    dual_hbm,
    out,
    near,
    gram,
    prolong,
    dual,
    near_field,
    rim_out,
    rim_in,
    mapped,
    fine_out,
    fine,
    load_sem,
    rim_send,
    rim_recv,
    rim_pass_send,
    rim_pass_recv,
    map_send,
    map_recv,
    fine_send,
    fine_recv,
    fine_pass_send,
    fine_pass_recv,
):
    near_terms, half_rows = near_cols.shape
    coarse, per, block, _ = prolong.shape
    terms = dual_cols.shape[0]
    columns = incident.shape[0]
    rim = primal_border.shape[2]
    rim_half = rim // 2
    fine_rim = fine_border.shape[2]
    fine_half = fine_rim // 2
    step = fine_half // CHUNKS
    own_fine = coarse * per
    row = lax.axis_index("row")
    surf = lax.axis_index("surf")
    sibling = {"row": 1 - row}
    neighbours = (
        {"surf": lax.rem(surf + parts - 1, parts)},
        {"surf": lax.rem(surf + 1, parts)},
    )

    moves = [(gram_hbm, gram), (near_hbm, near)]
    moves += [(prolong_hbm.at[:, :, pl.ds(j * block, block)], prolong.at[:, j]) for j in range(per)]
    moves += [(dual_hbm, dual)]
    loads = [
        pltpu.make_async_copy(src, dst, load_sem.at[i]) for i, (src, dst) in enumerate(moves)
    ]
    for load in loads:
        load.start()

    barrier = pltpu.get_barrier_semaphore()
    for device in neighbours + (sibling,):
        pl.semaphore_signal(barrier, inc=1, device_id=device, device_id_type=MESH)

    def lay(j, carry):
        near_field[j] = incident[:, pl.ds(pl.multiple_of(j * block, block), block)]
        return carry

    lax.fori_loop(0, coarse, lay, 0, unroll=4)
    for way in range(2):

        def pack(j, carry, way=way):
            at = primal_border[0, way, row * rim_half + j]
            rim_out[way, j] = near_field[at]
            return carry

        lax.fori_loop(0, rim_half, pack, 0, unroll=True)

    pl.semaphore_wait(barrier, 3)

    rim_copies = [
        pltpu.make_async_remote_copy(
            src_ref=rim_out.at[way],
            dst_ref=rim_in.at[1 - way, row],
            send_sem=rim_send.at[way],
            recv_sem=rim_recv.at[1 - way],
            device_id=neighbours[way],
            device_id_type=MESH,
        )
        for way in range(2)
    ]
    for copy in rim_copies:
        copy.start()

    fine[own_fine + 2 * fine_rim] = jnp.zeros((columns, block), jnp.bfloat16)

    loads[0].wait()
    loads[1].wait()

    def combine_near(i, carry):
        joined = dot(near[i].reshape(near_terms * block, block), gram[i]).astype(jnp.bfloat16)
        near[i] = joined.reshape(near_terms, block, block)
        return carry

    lax.fori_loop(0, half_rows, combine_near, 0, unroll=2)

    rim_passes = []
    for way in range(2):
        rim_copies[way].wait_recv()
        copy = pltpu.make_async_remote_copy(
            src_ref=rim_in.at[1 - way, row],
            dst_ref=rim_in.at[1 - way, row],
            send_sem=rim_pass_send.at[way],
            recv_sem=rim_pass_recv.at[way],
            device_id=sibling,
            device_id_type=MESH,
        )
        copy.start()
        rim_passes.append(copy)
    for copy in rim_passes:
        copy.wait_recv()
    for side in range(2):
        for half in range(2):
            for j in range(rim_half):
                near_field[coarse + side * rim + half * rim_half + j] = rim_in[side, half, j]

    map_copies = []
    map_step = half_rows // CHUNKS
    for chunk in range(CHUNKS):

        def primal(i, carry):
            picked = jnp.concatenate([near_field[near_cols[k, i]] for k in range(near_terms)], axis=1)
            mapped[row * half_rows + i] = dot(
                picked, near[i].reshape(near_terms * block, block)
            ).astype(jnp.bfloat16)
            return carry

        lax.fori_loop(chunk * map_step, (chunk + 1) * map_step, primal, 0, unroll=4)
        span = pl.ds(row * half_rows + chunk * map_step, map_step)
        copy = pltpu.make_async_remote_copy(
            src_ref=mapped.at[span],
            dst_ref=mapped.at[span],
            send_sem=map_send.at[chunk],
            recv_sem=map_recv.at[chunk],
            device_id=sibling,
            device_id_type=MESH,
        )
        copy.start()
        map_copies.append(copy)

    for load in loads[2:-1]:
        load.wait()
    for copy in map_copies:
        copy.wait()

    fine_copies = []
    for chunk in range(CHUNKS):
        for way in range(2):

            def border(j, carry, way=way):
                at = fine_border[0, way, row * fine_half + j]
                source = lax.div(at, per)
                fine_out[way, j] = dot(
                    mapped[source], prolong[source, at - source * per]
                ).astype(jnp.bfloat16)
                return carry

            lax.fori_loop(chunk * step, (chunk + 1) * step, border, 0, unroll=4)
            copy = pltpu.make_async_remote_copy(
                src_ref=fine_out.at[way, pl.ds(chunk * step, step)],
                dst_ref=fine.at[
                    pl.ds(own_fine + (1 - way) * fine_rim + row * fine_half + chunk * step, step)
                ],
                send_sem=fine_send.at[way, chunk],
                recv_sem=fine_recv.at[1 - way, chunk],
                device_id=neighbours[way],
                device_id_type=MESH,
            )
            copy.start()
            fine_copies.append((way, chunk, copy))

    def refine(q, carry):
        result = dot(mapped[q], spread(prolong, q)).astype(jnp.bfloat16)
        for j in range(per):
            fine[q * per + j] = result[:, j * block : (j + 1) * block]
        return carry

    lax.fori_loop(0, coarse, refine, 0, unroll=2)
    loads[-1].wait()

    def combine_dual(i, carry):
        back = dot(gram[i], spread(prolong, row * half_rows + i)).astype(jnp.bfloat16)
        for j in range(per):
            f = i * per + j
            joined = dot_t(
                dual[f].reshape(terms * block, block), back[:, j * block : (j + 1) * block]
            ).astype(jnp.bfloat16)
            dual[f] = joined.reshape(terms, block, block)
        return carry

    lax.fori_loop(0, half_rows, combine_dual, 0)

    fine_passes = []
    for way, chunk, arrived in fine_copies:
        arrived.wait_recv()
        span = pl.ds(own_fine + (1 - way) * fine_rim + row * fine_half + chunk * step, step)
        copy = pltpu.make_async_remote_copy(
            src_ref=fine.at[span],
            dst_ref=fine.at[span],
            send_sem=fine_pass_send.at[way, chunk],
            recv_sem=fine_pass_recv.at[way, chunk],
            device_id=sibling,
            device_id_type=MESH,
        )
        copy.start()
        fine_passes.append(copy)
    for copy in fine_passes:
        copy.wait()

    spare = own_fine + 2 * fine_rim

    def collapse(i, carry):
        picked = []
        for j in range(per):
            f = i * per + j
            live = dual_count[f]
            picked += [fine[pick(dual_cols[k, f], live, k, spare)] for k in range(terms)]
        joined = dual[pl.ds(i * per, per)].reshape(per * terms * block, block)
        out[:, pl.ds(pl.multiple_of(i * block, block), block)] = dot(
            jnp.concatenate(picked, axis=1), joined
        )
        return carry

    lax.fori_loop(0, half_rows, collapse, 0, unroll=2)

    for copy in rim_copies + rim_passes:
        copy.wait_send()
    for _, _, copy in fine_copies:
        copy.wait_send()


def body(
    parts,
    incident,
    near_blocks,
    near_cols,
    gram_inv,
    prolong,
    dual_blocks,
    dual_cols,
    dual_count,
    primal_border,
    fine_border,
):
    columns = incident.shape[0]
    coarse, block, wide = prolong.shape
    per = wide // block
    half_rows = near_blocks.shape[0]
    rim = primal_border.shape[2]
    fine_rim = fine_border.shape[2]
    cell = (columns, block)
    low = jnp.bfloat16
    smem = pl.BlockSpec(memory_space=pltpu.SMEM)
    vmem = pl.BlockSpec(memory_space=pltpu.VMEM)
    hbm = pl.BlockSpec(memory_space=pl.ANY)
    sems = pltpu.SemaphoreType.DMA
    return pl.pallas_call(
        functools.partial(kernel, parts),
        out_shape=jax.ShapeDtypeStruct((columns, half_rows * block), jnp.float32),
        in_specs=[smem] * 5 + [vmem] + [hbm] * 4,
        out_specs=vmem,
        scratch_shapes=[
            pltpu.VMEM(near_blocks.shape, low),
            pltpu.VMEM(gram_inv.shape, low),
            pltpu.VMEM((coarse, per, block, block), low),
            pltpu.VMEM(dual_blocks.shape, low),
            pltpu.VMEM((coarse + 2 * rim,) + cell, low),
            pltpu.VMEM((2, rim // 2) + cell, low),
            pltpu.VMEM((2, 2, rim // 2) + cell, low),
            pltpu.VMEM((coarse,) + cell, low),
            pltpu.VMEM((2, fine_rim // 2) + cell, low),
            pltpu.VMEM((coarse * per + 2 * fine_rim + 1,) + cell, low),
            sems((3 + per,)),
            sems((2,)),
            sems((2,)),
            sems((2,)),
            sems((2,)),
            sems((CHUNKS,)),
            sems((CHUNKS,)),
            sems((2, CHUNKS)),
            sems((2, CHUNKS)),
            sems((2, CHUNKS)),
            sems((2, CHUNKS)),
        ],
        compiler_params=pltpu.CompilerParams(
            collective_id=0, has_side_effects=True, vmem_limit_bytes=60 * 2**20
        ),
    )(
        near_cols.T,
        dual_cols.T,
        dual_count,
        primal_border,
        fine_border,
        incident,
        near_blocks,
        gram_inv,
        prolong,
        dual_blocks,
    )


def solution(mesh):
    return jax.shard_map(
        functools.partial(body, mesh.shape["surf"]),
        mesh=mesh,
        in_specs=(
            P(("grp", "ang"), "surf"),
            P(("grp", "surf", "row"), None, None, None),
            P(("grp", "surf", "row"), None),
            P(("grp", "surf", "row"), None, None),
            P(("grp", "surf"), None, None),
            P(("grp", "surf", "row"), None, None, None),
            P(("grp", "surf", "row"), None),
            P(("grp", "surf", "row")),
            P(("grp", "surf"), None, None),
            P(("grp", "surf"), None, None),
        ),
        out_specs=P(("grp", "ang"), ("surf", "row")),
        check_vma=False,
    )
```

```python
import functools

import jax
import jax.numpy as jnp
from jax import lax
from jax.experimental import pallas as pl
from jax.experimental.pallas import tpu as pltpu
from jax.sharding import PartitionSpec as P

MESH = pl.DeviceIdType.MESH
CHUNKS = 6
MAP_CHUNKS = 4
OUT_CHUNKS = 4


def dot(a, b):
    return jnp.dot(a, b, preferred_element_type=jnp.float32)


def dot_t(a, b):
    return lax.dot_general(a, b, (((1,), (1,)), ((), ())), preferred_element_type=jnp.float32)


def spread(prolong, q):
    return jnp.concatenate([prolong[q, j] for j in range(prolong.shape[1])], axis=1)


def pick(index, live, k, spare):
    if k == 0:
        return index
    return spare + (index - spare) * lax.min(lax.max(live - k, 0), 1)


def kernel(
    parts,
    near_cols_hbm,
    dual_cols_hbm,
    dual_count_hbm,
    primal_border,
    fine_border_hbm,
    incident_hbm,
    near_hbm,
    gram_hbm,
    prolong_hbm,
    dual_hbm,
    out_hbm,
    near_cols,
    dual_cols,
    dual_count,
    fine_border,
    incident,
    out,
    near,
    gram,
    prolong,
    dual,
    near_field,
    rim_out,
    rim_in,
    mapped,
    fine_out,
    fine,
    load_sem,
    table_sem,
    out_sem,
    rim_send,
    rim_recv,
    rim_pass_send,
    rim_pass_recv,
    map_send,
    map_recv,
    fine_send,
    fine_recv,
    fine_pass_send,
    fine_pass_recv,
):
    near_terms, half_rows = near_cols.shape
    coarse, per, block, _ = prolong.shape
    terms = dual_cols.shape[0]
    columns = incident.shape[0]
    rim = primal_border.shape[2]
    rim_half = rim // 2
    fine_rim = fine_border.shape[2]
    fine_half = fine_rim // 2
    step = fine_half // CHUNKS
    own_fine = coarse * per
    row = lax.axis_index("row")
    surf = lax.axis_index("surf")
    sibling = {"row": 1 - row}
    neighbours = (
        {"surf": lax.rem(surf + parts - 1, parts)},
        {"surf": lax.rem(surf + 1, parts)},
    )

    barrier = pltpu.get_barrier_semaphore()
    for device in neighbours + (sibling,):
        pl.semaphore_signal(barrier, inc=1, device_id=device, device_id_type=MESH)

    opening = pltpu.make_async_copy(incident_hbm, incident, table_sem.at[0])
    opening.start()
    tables = [
        pltpu.make_async_copy(src, dst, table_sem.at[1 + i])
        for i, (src, dst) in enumerate(
            (
                (near_cols_hbm, near_cols),
                (fine_border_hbm, fine_border),
                (dual_cols_hbm, dual_cols),
                (dual_count_hbm, dual_count),
            )
        )
    ]
    for table in tables:
        table.start()

    moves = [(gram_hbm, gram), (near_hbm, near)]
    moves += [(prolong_hbm.at[:, :, pl.ds(j * block, block)], prolong.at[:, j]) for j in range(per)]
    moves += [(dual_hbm, dual)]
    loads = [
        pltpu.make_async_copy(src, dst, load_sem.at[i]) for i, (src, dst) in enumerate(moves)
    ]
    for load in loads:
        load.start()

    opening.wait()

    def lay(j, carry):
        near_field[j] = incident[:, pl.ds(pl.multiple_of(j * block, block), block)]
        return carry

    lax.fori_loop(0, coarse, lay, 0, unroll=4)
    for way in range(2):

        def pack(j, carry, way=way):
            at = primal_border[0, way, row * rim_half + j]
            rim_out[way, j] = near_field[at]
            return carry

        lax.fori_loop(0, rim_half, pack, 0, unroll=True)

    pl.semaphore_wait(barrier, 3)

    rim_copies = [
        pltpu.make_async_remote_copy(
            src_ref=rim_out.at[way],
            dst_ref=rim_in.at[1 - way, row],
            send_sem=rim_send.at[way],
            recv_sem=rim_recv.at[1 - way],
            device_id=neighbours[way],
            device_id_type=MESH,
        )
        for way in range(2)
    ]
    for copy in rim_copies:
        copy.start()

    fine[own_fine + 2 * fine_rim] = jnp.zeros((columns, block), jnp.bfloat16)

    loads[0].wait()
    loads[1].wait()

    def combine_near(i, carry):
        joined = dot(near[i].reshape(near_terms * block, block), gram[i]).astype(jnp.bfloat16)
        near[i] = joined.reshape(near_terms, block, block)
        return carry

    lax.fori_loop(0, half_rows, combine_near, 0, unroll=2)

    rim_passes = []
    for way in range(2):
        rim_copies[way].wait_recv()
        copy = pltpu.make_async_remote_copy(
            src_ref=rim_in.at[1 - way, row],
            dst_ref=rim_in.at[1 - way, row],
            send_sem=rim_pass_send.at[way],
            recv_sem=rim_pass_recv.at[way],
            device_id=sibling,
            device_id_type=MESH,
        )
        copy.start()
        rim_passes.append(copy)
    for copy in rim_passes:
        copy.wait_recv()
    for side in range(2):
        for half in range(2):
            for j in range(rim_half):
                near_field[coarse + side * rim + half * rim_half + j] = rim_in[side, half, j]

    for table in tables:
        table.wait()
    map_copies = []
    map_step = half_rows // MAP_CHUNKS
    for chunk in range(MAP_CHUNKS):

        def primal(i, carry):
            picked = jnp.concatenate([near_field[near_cols[k, i]] for k in range(near_terms)], axis=1)
            mapped[row * half_rows + i] = dot(
                picked, near[i].reshape(near_terms * block, block)
            ).astype(jnp.bfloat16)
            return carry

        lax.fori_loop(chunk * map_step, (chunk + 1) * map_step, primal, 0, unroll=4)
        span = pl.ds(row * half_rows + chunk * map_step, map_step)
        copy = pltpu.make_async_remote_copy(
            src_ref=mapped.at[span],
            dst_ref=mapped.at[span],
            send_sem=map_send.at[chunk],
            recv_sem=map_recv.at[chunk],
            device_id=sibling,
            device_id_type=MESH,
        )
        copy.start()
        map_copies.append(copy)

    for load in loads[2:-1]:
        load.wait()
    for copy in map_copies:
        copy.wait()

    fine_copies = []
    for chunk in range(CHUNKS):
        for way in range(2):

            def border(j, carry, way=way):
                at = fine_border[0, way, row * fine_half + j]
                source = lax.div(at, per)
                fine_out[way, j] = dot(
                    mapped[source], prolong[source, at - source * per]
                ).astype(jnp.bfloat16)
                return carry

            lax.fori_loop(chunk * step, (chunk + 1) * step, border, 0, unroll=4)
            copy = pltpu.make_async_remote_copy(
                src_ref=fine_out.at[way, pl.ds(chunk * step, step)],
                dst_ref=fine.at[
                    pl.ds(own_fine + (1 - way) * fine_rim + row * fine_half + chunk * step, step)
                ],
                send_sem=fine_send.at[way, chunk],
                recv_sem=fine_recv.at[1 - way, chunk],
                device_id=neighbours[way],
                device_id_type=MESH,
            )
            copy.start()
            fine_copies.append((way, chunk, copy))

    def refine(q, carry):
        result = dot(mapped[q], spread(prolong, q)).astype(jnp.bfloat16)
        for j in range(per):
            fine[q * per + j] = result[:, j * block : (j + 1) * block]
        return carry

    lax.fori_loop(0, coarse, refine, 0, unroll=2)
    loads[-1].wait()

    def combine_dual(i, carry):
        back = dot(gram[i], spread(prolong, row * half_rows + i)).astype(jnp.bfloat16)
        for j in range(per):
            f = i * per + j
            joined = dot_t(
                dual[f].reshape(terms * block, block), back[:, j * block : (j + 1) * block]
            ).astype(jnp.bfloat16)
            dual[f] = joined.reshape(terms, block, block)
        return carry

    lax.fori_loop(0, half_rows, combine_dual, 0)

    fine_passes = []
    for way, chunk, arrived in fine_copies:
        arrived.wait_recv()
        span = pl.ds(own_fine + (1 - way) * fine_rim + row * fine_half + chunk * step, step)
        copy = pltpu.make_async_remote_copy(
            src_ref=fine.at[span],
            dst_ref=fine.at[span],
            send_sem=fine_pass_send.at[way, chunk],
            recv_sem=fine_pass_recv.at[way, chunk],
            device_id=sibling,
            device_id_type=MESH,
        )
        copy.start()
        fine_passes.append(copy)
    for copy in fine_passes:
        copy.wait()

    spare = own_fine + 2 * fine_rim

    def collapse(i, carry):
        picked = []
        for j in range(per):
            f = i * per + j
            live = dual_count[f]
            picked += [fine[pick(dual_cols[k, f], live, k, spare)] for k in range(terms)]
        joined = dual[pl.ds(i * per, per)].reshape(per * terms * block, block)
        out[:, pl.ds(pl.multiple_of(i * block, block), block)] = dot(
            jnp.concatenate(picked, axis=1), joined
        )
        return carry

    out_step = half_rows // OUT_CHUNKS
    results = []
    for chunk in range(OUT_CHUNKS):
        lax.fori_loop(chunk * out_step, (chunk + 1) * out_step, collapse, 0, unroll=4)
        span = pl.ds(chunk * out_step * block, out_step * block)
        result = pltpu.make_async_copy(out.at[:, span], out_hbm.at[:, span], out_sem.at[chunk])
        result.start()
        results.append(result)

    for copy in rim_copies + rim_passes:
        copy.wait_send()
    for _, _, copy in fine_copies:
        copy.wait_send()
    for result in results:
        result.wait()


def body(
    parts,
    incident,
    near_blocks,
    near_cols,
    gram_inv,
    prolong,
    dual_blocks,
    dual_cols,
    dual_count,
    primal_border,
    fine_border,
):
    columns = incident.shape[0]
    coarse, block, wide = prolong.shape
    per = wide // block
    half_rows = near_blocks.shape[0]
    rim = primal_border.shape[2]
    fine_rim = fine_border.shape[2]
    cell = (columns, block)
    low = jnp.bfloat16
    smem = pl.BlockSpec(memory_space=pltpu.SMEM)
    hbm = pl.BlockSpec(memory_space=pl.ANY)
    sems = pltpu.SemaphoreType.DMA
    return pl.pallas_call(
        functools.partial(kernel, parts),
        out_shape=jax.ShapeDtypeStruct((columns, half_rows * block), jnp.float32),
        in_specs=[hbm] * 3 + [smem] + [hbm] * 6,
        out_specs=hbm,
        scratch_shapes=[
            pltpu.SMEM(near_cols.shape[::-1], jnp.int32),
            pltpu.SMEM(dual_cols.shape[::-1], jnp.int32),
            pltpu.SMEM(dual_count.shape, jnp.int32),
            pltpu.SMEM(fine_border.shape, jnp.int32),
            pltpu.VMEM(incident.shape, low),
            pltpu.VMEM((columns, half_rows * block), jnp.float32),
            pltpu.VMEM(near_blocks.shape, low),
            pltpu.VMEM(gram_inv.shape, low),
            pltpu.VMEM((coarse, per, block, block), low),
            pltpu.VMEM(dual_blocks.shape, low),
            pltpu.VMEM((coarse + 2 * rim,) + cell, low),
            pltpu.VMEM((2, rim // 2) + cell, low),
            pltpu.VMEM((2, 2, rim // 2) + cell, low),
            pltpu.VMEM((coarse,) + cell, low),
            pltpu.VMEM((2, fine_rim // 2) + cell, low),
            pltpu.VMEM((coarse * per + 2 * fine_rim + 1,) + cell, low),
            sems((3 + per,)),
            sems((5,)),
            sems((OUT_CHUNKS,)),
            sems((2,)),
            sems((2,)),
            sems((2,)),
            sems((2,)),
            sems((MAP_CHUNKS,)),
            sems((MAP_CHUNKS,)),
            sems((2, CHUNKS)),
            sems((2, CHUNKS)),
            sems((2, CHUNKS)),
            sems((2, CHUNKS)),
        ],
        compiler_params=pltpu.CompilerParams(
            collective_id=0, has_side_effects=True, vmem_limit_bytes=60 * 2**20
        ),
    )(
        near_cols.T,
        dual_cols.T,
        dual_count,
        primal_border,
        fine_border,
        incident,
        near_blocks,
        gram_inv,
        prolong,
        dual_blocks,
    )


def solution(mesh):
    return jax.shard_map(
        functools.partial(body, mesh.shape["surf"]),
        mesh=mesh,
        in_specs=(
            P(("grp", "ang"), "surf"),
            P(("grp", "surf", "row"), None, None, None),
            P(("grp", "surf", "row"), None),
            P(("grp", "surf", "row"), None, None),
            P(("grp", "surf"), None, None),
            P(("grp", "surf", "row"), None, None, None),
            P(("grp", "surf", "row"), None),
            P(("grp", "surf", "row")),
            P(("grp", "surf"), None, None),
            P(("grp", "surf"), None, None),
        ),
        out_specs=P(("grp", "ang"), ("surf", "row")),
        check_vma=False,
    )
```
